32 devices in a mesh: pairs: 8 (over y, x, core), day: 4 (over z).
Axes of the slice: x: 2, y: 2, z: 4, core: 2. Of those that a mesh axis runs over, the one named last changes fastest.
Arguments:
- spectra: bfloat16 [4, 2, 256, 18432], P('day', None, 'pairs'), may hold values from -6 to 6
- station_row: int32 [256], replicated, may hold values from 0 to 255, as said below
- needed: int32 [128], P('pairs'), may hold values from 0 to 255, as said below
- pair_list: int32 [512, 2], P('pairs'), may hold values from 0 to 15, as said below
- counts: int32 [8], P('pairs'), may hold values from 32 to 64, as said below
Outputs:
- correlations: float32 [512, 1024], P(('pairs', 'day'))
The draws below stay inside these ranges and needn't reach their ends.
Inputs may be any that keep to these rules, and one draw needn't show every extreme that they name: `station_row`: A permutation of the stations: each row of the spectra belongs to exactly one station. `needed`: each block's 16 entries are distinct stations; at most 4 of one block's stations have their rows on any one index of pairs, and in every block some index of pairs holds exactly 4 of them. `pair_list`: the two positions of a slot differ; empty slots also hold valid positions. `counts`: the live slots of a block are its first ones; in every draw some block has all 64 slots live.
All inputs are finite; a program needn't handle non-finite values.
Results may differ from the reference program's by a relative error of at most 0.013.
Values may be sent and summed in bfloat16 or wider, within the bound.
A program may use at most 128 MiB of HBM per device.

```python
import math
import jax
import jax.numpy as jnp
from jax import lax

F = 18432
LAGS = 1024
KLO = 720
NFFT = 72000
CAP = 4
STA_DEV = 32
PAIR_DEV = 64
NEED = 16
S = 256
DAYS = 4
PAIRS = 512


def draw_spectra(key, part):
    key_noise, key_common, key_group, key_jitter = jax.random.split(jax.random.fold_in(key, 15), 4)
    noise_part = jnp.clip(jax.random.normal(key_noise, (DAYS, 2, S, F), jnp.float32), -5.0, 5.0)
    common_part = jnp.clip(jax.random.normal(key_common, (DAYS, 2, 1, F), jnp.float32), -4.0, 4.0)
    station_group = jax.random.randint(key_group, (S,), 0, 2).astype(jnp.int32)
    station_jitter = jax.random.randint(key_jitter, (S,), 0, max(LAGS // 32, 1)).astype(jnp.int32)
    station_delay = station_group * (21 * LAGS // 32) + station_jitter
    bins_here = KLO + jnp.arange(F, dtype=jnp.int32)
    phase_angle = jnp.mod(station_delay[:, None] * bins_here[None, :], NFFT).astype(jnp.float32) * (2.0 * math.pi / NFFT)
    cosine = jnp.cos(phase_angle)[None, :, :]
    sine_part = jnp.sin(phase_angle)[None, :, :]
    shifted_real = common_part[:, 0] * cosine + common_part[:, 1] * sine_part
    shifted_imag = common_part[:, 1] * cosine - common_part[:, 0] * sine_part
    signal = jnp.stack([shifted_real, shifted_imag], axis=1)
    return jnp.clip(noise_part + 0.35 * signal, -6.0, 6.0).astype(jnp.bfloat16)


def shuffled_rows(key):
    return jax.random.permutation(jax.random.fold_in(key, 11), S).astype(jnp.int32)


def draw_station_row(key, part):
    return shuffled_rows(key)


def draw_needed(key, part):
    holders = S // STA_DEV
    rows_of = shuffled_rows(key)
    station_at = jnp.argsort(rows_of, stable=True).astype(jnp.int32)
    block_keys = jax.random.split(jax.random.fold_in(key, 12), holders)

    def one_block(block_key):
        key_split, key_holder, key_local, key_order = jax.random.split(block_key, 4)
        lower = jax.random.randint(key_split, (holders // 2,), 0, CAP // 2 + 1).astype(jnp.int32)
        lower = lower.at[0].set(0)
        loads = jnp.stack([CAP - lower, lower], axis=1).reshape(holders)
        loads = loads[jax.random.permutation(key_holder, holders)]
        scores = jax.random.randint(key_local, (holders, STA_DEV), 0, 1 << 20).astype(jnp.int32) * STA_DEV + jnp.arange(STA_DEV, dtype=jnp.int32)[None, :]
        local_rows = jnp.argsort(scores, axis=1, stable=True)[:, :CAP].astype(jnp.int32)
        global_rows = (jnp.arange(holders, dtype=jnp.int32)[:, None] * STA_DEV + local_rows).reshape(-1)
        valid = (jnp.arange(CAP, dtype=jnp.int32)[None, :] < loads[:, None]).reshape(-1)
        order_scores = jnp.where(valid, 0, 1).astype(jnp.int32) * (1 << 24) + jax.random.randint(key_order, (holders * CAP,), 0, 1 << 16).astype(jnp.int32) * (holders * CAP) + jnp.arange(holders * CAP, dtype=jnp.int32)
        picked = jnp.argsort(order_scores, stable=True)[:NEED]
        return station_at[global_rows[picked]]
    return jax.vmap(one_block)(block_keys).reshape(-1).astype(jnp.int32)


def draw_pair_list(key, part):
    key_first, key_offset = jax.random.split(jax.random.fold_in(key, 13))
    first = jax.random.randint(key_first, (PAIRS,), 0, NEED).astype(jnp.int32)
    offset = jax.random.randint(key_offset, (PAIRS,), 1, NEED).astype(jnp.int32)
    second = jnp.mod(first + offset, NEED).astype(jnp.int32)
    return jnp.stack([first, second], axis=1)


def draw_counts(key, part):
    blocks = S // STA_DEV
    key_count, key_full = jax.random.split(jax.random.fold_in(key, 14))
    values = jax.random.randint(key_count, (blocks,), PAIR_DEV // 2, PAIR_DEV + 1).astype(jnp.int32)
    full_block = jax.random.randint(key_full, (), 0, blocks).astype(jnp.int32)
    return jnp.where(jnp.arange(blocks, dtype=jnp.int32) == full_block, PAIR_DEV, values).astype(jnp.int32)


def setup_inputs(seed: int = 0) -> dict:
    key_of = jax.random.split(jax.random.key(seed), 6)
    spectra = draw_spectra(jax.random.fold_in(key_of[5], 71), 0)
    station_row = draw_station_row(jax.random.fold_in(key_of[5], 71), 0)
    needed = draw_needed(jax.random.fold_in(key_of[5], 71), 0)
    pair_list = draw_pair_list(jax.random.fold_in(key_of[5], 71), 0)
    counts = draw_counts(jax.random.fold_in(key_of[5], 71), 0)
    return {"spectra": spectra, "station_row": station_row, "needed": needed, "pair_list": pair_list, "counts": counts}


def lag_tables():
    bins_here = KLO + jnp.arange(F, dtype=jnp.int32)
    shifts = jnp.arange(LAGS, dtype=jnp.int32) - LAGS // 2
    phases = jnp.mod(bins_here[:, None] * shifts[None, :], NFFT).astype(jnp.float32) * (2.0 * math.pi / NFFT)
    cosine = jnp.cos(phases).astype(jnp.bfloat16).astype(jnp.float32)
    sine = jnp.sin(phases).astype(jnp.bfloat16).astype(jnp.float32)
    return (cosine, sine)

def wire_round(values):
    rounded = lax.optimization_barrier(values.astype(jnp.bfloat16))
    return rounded.astype(jnp.float32)

def reference(spectra, station_row, needed, pair_list, counts):
    days = spectra.shape[0]
    blocks = counts.shape[0]
    cosine, sine = lag_tables()

    def one_block(block):
        names = lax.dynamic_slice_in_dim(needed, (block * NEED).astype(jnp.int32), NEED, 0)
        rows_here = station_row[names]
        spec_here = jnp.take(spectra, rows_here, axis=2)
        slots = lax.dynamic_slice_in_dim(pair_list, (block * PAIR_DEV).astype(jnp.int32), PAIR_DEV, 0)
        first = jnp.take(spec_here, slots[:, 0], axis=2).astype(jnp.float32)
        second = jnp.take(spec_here, slots[:, 1], axis=2).astype(jnp.float32)
        cross_real = first[:, 0] * second[:, 0] + first[:, 1] * second[:, 1]
        cross_imag = first[:, 1] * second[:, 0] - first[:, 0] * second[:, 1]
        divisor = jnp.maximum(jnp.sqrt(cross_real * cross_real + cross_imag * cross_imag), 0.25)
        unit_real = cross_real / divisor
        unit_imag = cross_imag / divisor
        sum_real = lax.optimization_barrier(jnp.sum(wire_round(cross_real), axis=0))
        sum_imag = lax.optimization_barrier(jnp.sum(wire_round(cross_imag), axis=0))
        usum_real = lax.optimization_barrier(jnp.sum(wire_round(unit_real), axis=0))
        usum_imag = lax.optimization_barrier(jnp.sum(wire_round(unit_imag), axis=0))
        live = (jnp.arange(PAIR_DEV, dtype=jnp.int32) < counts[block]).astype(jnp.float32)[:, None]
        coherence = (usum_real * usum_real + usum_imag * usum_imag) / (days * days)
        factor = coherence * live
        stack_real = (sum_real / days * factor).astype(jnp.bfloat16).astype(jnp.float32)
        stack_imag = (sum_imag / days * factor).astype(jnp.bfloat16).astype(jnp.float32)
        total = jnp.dot(stack_real, cosine, precision=lax.Precision.HIGHEST, preferred_element_type=jnp.float32)
        total = total - jnp.dot(stack_imag, sine, precision=lax.Precision.HIGHEST, preferred_element_type=jnp.float32)
        return total * (8.0 / math.sqrt(F))
    result = lax.map(one_block, jnp.arange(blocks, dtype=jnp.int32))
    return result.reshape(blocks * PAIR_DEV, LAGS)
```

```python
import functools
import math

import jax
import jax.numpy as jnp
import numpy as np
from jax import lax
from jax.experimental import pallas as pl
from jax.experimental.pallas import tpu as pltpu
from jax.sharding import PartitionSpec as P

LAGS = 1024
KLO = 720
NFFT = 72000
CAP = 4
HALF = LAGS // 2
FLOOR = 0.25
MESH = pl.DeviceIdType.MESH


def lag_constants(bins, days, block):
    odd = 2 * np.arange(HALF, dtype=np.int64) + 1

    def angle(steps):
        return (np.mod(steps, 2 * NFFT) * (math.pi / NFFT)).astype(np.float64)

    inner = angle(np.arange(block, dtype=np.int64)[:, None] * odd[None, :])
    table = np.concatenate([np.cos(inner), np.sin(inner)], axis=1).astype(jnp.bfloat16)
    starts = KLO + np.arange(0, bins, block, dtype=np.int64)
    outer = angle(starts[:, None] * odd[None, :])
    outer = np.stack([np.cos(outer), np.sin(outer)], axis=1).astype(np.float32)
    turn = angle(KLO + np.arange(bins, dtype=np.int64))
    turn = np.stack([np.cos(turn), np.sin(turn)]).astype(np.float32)
    turn = turn.reshape(2, days, bins // days).transpose(1, 0, 2)
    return table, outer.reshape(days, -1, 2, HALF), turn


def kernel(
    holders, days, spec, req, comp, sel, table, outer, turn, out,
    reqin, outbox, inbox, zout, zin, stack, even, odd, part, shares,
    qsend, qrecv, xsend, xrecv, zsend, zrecv, rsend, rrecv,
):
    me, day = lax.axis_index("pairs"), lax.axis_index("day")
    width = outbox.shape[2]
    need4 = zin.shape[1]
    slots = part.shape[0]
    share = slots // days
    block = table.shape[0]
    tile = 256 if block % 256 == 0 else 128
    blocks = 2 * width // block

    def xy(p):
        return lax.rem(me + p, holders)

    def zz(s):
        return lax.rem(day + s, days)

    def rows16(b):
        return pl.ds(pl.multiple_of(b * 16, 16), 16)

    def remote(src, dst, ssem, rsem, dev):
        return pltpu.make_async_remote_copy(
            src_ref=src, dst_ref=dst, send_sem=ssem, recv_sem=rsem, device_id=dev, device_id_type=MESH
        )

    def ask(p):
        return remote(req.at[rows16(xy(p))], reqin.at[rows16(me)], qsend.at[p], qrecv.at[p], (xy(p), day))

    def give(f, p):
        return remote(
            outbox.at[f, rows16(xy(p))], inbox.at[f, rows16(me)], xsend.at[f, p], xrecv.at[f, p], (xy(p), day)
        )

    def pass_on(s):
        return remote(zout.at[zz(s)], zin.at[day], zsend.at[s], zrecv.at[s], (me, zz(s)))

    def hand(s):
        rows = pl.ds(pl.multiple_of(zz(s) * share, share), share)
        return remote(part.at[rows], shares.at[day], rsend.at[s], rrecv.at[s], (me, zz(s)))

    barrier = pltpu.get_barrier_semaphore()
    for p in range(1, holders):
        pl.semaphore_signal(barrier, inc=1, device_id=(xy(p), day), device_id_type=MESH)
    for s in range(1, days):
        pl.semaphore_signal(barrier, inc=1, device_id=(me, zz(s)), device_id_type=MESH)
    pl.semaphore_wait(barrier, holders + days - 2)

    for p in range(1, holders):
        ask(p).start()
    reqin[rows16(me)] = req[rows16(me)]
    for p in range(1, holders):
        ask(p).wait()
    lanes = lax.broadcasted_iota(jnp.int32, reqin.shape, 1)
    pick = jnp.where(reqin[...] == lanes, 1.0, 0.0).astype(jnp.bfloat16)

    def send_step(step, carry):
        f = lax.rem(day + 1 + step, days)
        parts = []
        for h in range(2):
            cols = pl.ds(pl.multiple_of((2 * f + h) * width, 128), width)
            for c in range(2):
                parts.append(spec[c, :, cols])
        picked = jnp.dot(pick, jnp.concatenate(parts, axis=0), preferred_element_type=jnp.float32)
        outbox[f] = picked.astype(jnp.bfloat16)
        for p in range(1, holders):
            give(f, p).start()
        inbox[f, rows16(me)] = outbox[f, rows16(me)]
        return carry

    lax.fori_loop(0, days, send_step, 0)

    for s in range(1, days + 1):
        f = zz(s)
        for p in range(1, holders):
            give(f, p).wait_recv()
        packed = jnp.dot(comp[...], inbox[f], preferred_element_type=jnp.float32).astype(jnp.bfloat16)
        if s < days:
            zout[f] = packed
            pass_on(s).start()
        else:
            zin[day] = packed

    even[...] = jnp.zeros_like(even)
    odd[...] = jnp.zeros_like(odd)
    for s in range(1, days):
        pass_on(s).wait_recv()

    def block_step(n, carry):
        half = n // (blocks // 2)
        base = (n - half * (blocks // 2)) * block
        rows = pl.ds(pl.multiple_of(half * (need4 // 2), 16), need4 // 2)

        def tile_step(t, inner):
            cols = pl.ds(pl.multiple_of(base + t * tile, 128), tile)
            sums = None
            for d in range(days):
                both = jnp.dot(sel[...], zin[d, rows, cols], preferred_element_type=jnp.float32)
                a, b = both[:slots], both[slots : 2 * slots]
                c, e = both[2 * slots : 3 * slots], both[3 * slots :]
                real = a * c + b * e
                imag = b * c - a * e
                inv = lax.rsqrt(jnp.maximum(real * real + imag * imag, FLOOR * FLOOR))
                terms = (real, imag, real * inv, imag * inv)
                sums = terms if sums is None else tuple(x + y for x, y in zip(sums, terms))
            coherence = sums[2] * sums[2] + sums[3] * sums[3]
            real, imag = sums[0] * coherence, sums[1] * coherence
            at = pl.ds(pl.multiple_of(n * block + t * tile, 128), tile)
            cos, sin = turn[day, 0:1, at], turn[day, 1:2, at]
            to = pl.ds(pl.multiple_of(t * tile, 128), tile)
            stack[0:slots, to] = (real * cos + imag * sin).astype(jnp.bfloat16)
            stack[slots : 2 * slots, to] = (imag * cos - real * sin).astype(jnp.bfloat16)
            return inner

        lax.fori_loop(0, block // tile, tile_step, 0)
        z = jnp.dot(stack[...], table[...], preferred_element_type=jnp.float32)
        cos, sin = outer[day, n, 0:1, :], outer[day, n, 1:2, :]
        even[...] += cos * z[:slots, :HALF] - sin * z[:slots, HALF:]
        odd[...] += sin * z[slots:, :HALF] + cos * z[slots:, HALF:]
        return carry

    lax.fori_loop(0, blocks, block_step, 0)

    flip = lax.broadcasted_iota(jnp.int32, (HALF, HALF), 0) + lax.broadcasted_iota(jnp.int32, (HALF, HALF), 1)
    flip = jnp.where(flip == HALF - 1, 1.0, 0.0)
    part[:, HALF:] = even[...] - odd[...]
    part[:, :HALF] = jnp.dot(
        even[...] + odd[...], flip, precision=lax.Precision.HIGHEST, preferred_element_type=jnp.float32
    )
    for s in range(1, days):
        hand(s).start()
    shares[day] = part[pl.ds(pl.multiple_of(day * share, share), share)]
    for s in range(1, days):
        hand(s).wait_recv()
    total = shares[0]
    for d in range(1, days):
        total = total + shares[d]
    out[...] = total

    for s in range(1, days):
        hand(s).wait_send()
        pass_on(s).wait_send()
    for s in range(1, days + 1):
        for p in range(1, holders):
            give(zz(s), p).wait_send()


def shards(days, holders, spectra, station_row, needed, pair_list, counts):
    stations = spectra.shape[2]
    bins = spectra.shape[3]
    need = needed.shape[0]
    slots = pair_list.shape[0]
    width = bins // days // 2
    block = width // 3
    names = jnp.arange(station_row.shape[0], dtype=jnp.int32)
    my_rows = jnp.sum(jnp.where(needed[:, None] == names[None, :], station_row[None, :], 0), axis=1)
    owner = my_rows // stations
    local = my_rows % stations
    places = jnp.arange(need, dtype=jnp.int32)
    earlier = places[None, :] < places[:, None]
    rank = jnp.sum(jnp.logical_and(owner[:, None] == owner[None, :], earlier), axis=1).astype(jnp.int32)
    my_slot = owner * CAP + rank

    where_is = jnp.arange(holders * CAP, dtype=jnp.int32)
    asked = jnp.sum(jnp.where(where_is[:, None] == my_slot[None, :], local[None, :] + 1, 0), axis=1) - 1
    asked = asked.reshape(holders, 1, CAP)
    quarter = jnp.arange(4, dtype=jnp.int32)
    req = jnp.where(asked >= 0, quarter[None, :, None] * stations + asked, -1)
    req = jnp.broadcast_to(req.reshape(holders * 16, 1), (holders * 16, 4 * stations))

    comp = (owner * 16 + rank)[None, :] + (quarter * CAP)[:, None]
    comp = comp.reshape(4 * need, 1) == jnp.arange(holders * 16, dtype=jnp.int32)[None, :]
    comp = comp.astype(jnp.bfloat16)
    kinds = pair_list.T[:, None, :] + (jnp.arange(2, dtype=jnp.int32) * need)[None, :, None]
    sel = kinds.reshape(4 * slots, 1) == jnp.arange(2 * need, dtype=jnp.int32)[None, :]
    sel = sel.astype(jnp.bfloat16)

    table, outer, turn = lag_constants(bins, days, block)
    bf, f32 = jnp.bfloat16, jnp.float32
    dma = pltpu.SemaphoreType.DMA
    vmem = pl.BlockSpec(memory_space=pltpu.VMEM)
    summed = pl.pallas_call(
        functools.partial(kernel, holders, days),
        out_shape=jax.ShapeDtypeStruct((slots // days, LAGS), f32),
        in_specs=[vmem] * 7,
        out_specs=vmem,
        scratch_shapes=[
            pltpu.VMEM((holders * 16, 4 * stations), jnp.int32),
            pltpu.VMEM((days, holders * 16, width), bf),
            pltpu.VMEM((days, holders * 16, width), bf),
            pltpu.VMEM((days, 4 * need, width), bf),
            pltpu.VMEM((days, 4 * need, width), bf),
            pltpu.VMEM((2 * slots, block), bf),
            pltpu.VMEM((slots, HALF), f32),
            pltpu.VMEM((slots, HALF), f32),
            pltpu.VMEM((slots, LAGS), f32),
            pltpu.VMEM((days, slots // days, LAGS), f32),
            dma((holders,)), dma((holders,)),
            dma((days, holders)), dma((days, holders)),
            dma((days,)), dma((days,)),
            dma((days,)), dma((days,)),
        ],
        compiler_params=pltpu.CompilerParams(
            collective_id=0, has_side_effects=True, vmem_limit_bytes=48 * 2**20
        ),
    )(spectra[0], req, comp, sel, jnp.asarray(table), jnp.asarray(outer), jnp.asarray(turn))
    share = slots // days
    mine = lax.axis_index("day") * share + jnp.arange(share, dtype=jnp.int32)
    scale = 8.0 / math.sqrt(bins) / float(days) ** 3
    return jnp.where((mine < counts[0])[:, None], summed * scale, 0.0)


def solution(mesh):
    in_specs = (P("day", None, "pairs", None), P(), P("pairs"), P("pairs", None), P("pairs"))
    out_specs = P(("pairs", "day"), None)
    body = functools.partial(shards, mesh.shape["day"], mesh.shape["pairs"])
    return jax.shard_map(body, mesh=mesh, in_specs=in_specs, out_specs=out_specs, check_vma=False)
```

```python
import functools
import math

import jax
import jax.numpy as jnp
import numpy as np
from jax import lax
from jax.experimental import pallas as pl
from jax.experimental.pallas import tpu as pltpu
from jax.sharding import PartitionSpec as P

LAGS = 1024
KLO = 720
NFFT = 72000
CAP = 4
HALF = LAGS // 2
FLOOR = 0.25
CUTS = 3
AHEAD = 4
MESH = pl.DeviceIdType.MESH


def lag_constants(bins, days, block):
    odd = 2 * np.arange(HALF, dtype=np.int64) + 1

    def angle(steps):
        return (np.mod(steps, 2 * NFFT) * (math.pi / NFFT)).astype(np.float64)

    inner = angle(np.arange(block, dtype=np.int64)[:, None] * odd[None, :])
    table = np.concatenate([np.cos(inner), np.sin(inner)], axis=1).astype(jnp.bfloat16)
    starts = KLO + np.arange(0, bins, block, dtype=np.int64)
    outer = angle(starts[:, None] * odd[None, :])
    outer = np.stack([np.cos(outer), np.sin(outer)], axis=1).astype(np.float32)
    turn = angle(KLO + np.arange(bins, dtype=np.int64))
    turn = np.stack([np.cos(turn), np.sin(turn)]).astype(np.float32)
    turn = turn.reshape(2, days, bins // days).transpose(1, 0, 2)
    return table, outer.reshape(days, -1, 2, HALF), turn


def kernel(
    holders, days, cuts, spec_hbm, req, comp, sel, table_hbm, outer_hbm, turn_hbm, out,
    spec, table, outer, turn, reqin, outbox, inbox, zout, zin, stack, even, odd, flip, part, shares,
    lsem, qsend, qrecv, xsend, xrecv, zsend, zrecv, rsend, rrecv,
):
    me, day = lax.axis_index("pairs"), lax.axis_index("day")
    width = outbox.shape[2]
    need4 = zin.shape[2]
    slots = even.shape[0]
    share = slots // days
    units = cuts * days
    tile = 256 if width % 256 == 0 else 128

    def xy(p):
        return lax.rem(me + p, holders)

    def zz(s):
        return lax.rem(day + s, days)

    def rows16(b):
        return pl.ds(pl.multiple_of(b * 16, 16), 16)

    def remote(src, dst, ssem, rsem, dev):
        return pltpu.make_async_remote_copy(
            src_ref=src, dst_ref=dst, send_sem=ssem, recv_sem=rsem, device_id=dev, device_id_type=MESH
        )

    def ask(p):
        return remote(req.at[rows16(xy(p))], reqin.at[rows16(me)], qsend.at[p], qrecv.at[p], (xy(p), day))

    def give(i, p):
        return remote(
            outbox.at[i, rows16(xy(p))], inbox.at[i, rows16(me)], xsend.at[i, p], xrecv.at[i, p], (xy(p), day)
        )

    def pass_on(u, s):
        return remote(zout.at[u, s], zin.at[u, day], zsend.at[u, s], zrecv.at[u, s], (me, zz(s)))

    def hand(s):
        return remote(part.at[zz(s)], shares.at[day], rsend.at[s], rrecv.at[s], (me, zz(s)))

    loads = [
        pltpu.make_async_copy(src, dst, lsem.at[i])
        for i, (src, dst) in enumerate(
            ((spec_hbm, spec), (table_hbm, table), (outer_hbm, outer), (turn_hbm, turn))
        )
    ]
    for load in loads:
        load.start()

    barrier = pltpu.get_barrier_semaphore()
    for p in range(1, holders):
        pl.semaphore_signal(barrier, inc=1, device_id=(xy(p), day), device_id_type=MESH)
    for s in range(1, days):
        pl.semaphore_signal(barrier, inc=1, device_id=(me, zz(s)), device_id_type=MESH)
    pl.semaphore_wait(barrier, holders + days - 2)

    for p in range(1, holders):
        ask(p).start()
    reqin[rows16(me)] = req[rows16(me)]
    across = lax.broadcasted_iota(jnp.int32, (HALF, HALF), 0) + lax.broadcasted_iota(jnp.int32, (HALF, HALF), 1)
    flip[...] = jnp.where(across == HALF - 1, 1.0, 0.0).astype(jnp.bfloat16)
    even[...] = jnp.zeros_like(even)
    odd[...] = jnp.zeros_like(odd)
    loads[0].wait()
    for p in range(1, holders):
        ask(p).wait()
    lanes = lax.broadcasted_iota(jnp.int32, reqin.shape, 1)
    pick = jnp.where(reqin[...] == lanes, 1.0, 0.0).astype(jnp.bfloat16)

    def give_unit(i):
        u, s = i // days, i % days + 1
        parts = []
        for h in range(2):
            at = ((2 * zz(s) + h) * cuts + u) * width
            for c in range(2):
                parts.append(spec[c, :, pl.ds(pl.multiple_of(at, 128), width)])
        picked = jnp.dot(pick, jnp.concatenate(parts, axis=0), preferred_element_type=jnp.float32)
        outbox[i] = picked.astype(jnp.bfloat16)
        for p in range(1, holders):
            give(i, p).start()
        inbox[i, rows16(me)] = outbox[i, rows16(me)]

    def relay_unit(i):
        u, s = i // days, i % days + 1
        for p in range(1, holders):
            give(i, p).wait_recv()
        packed = jnp.dot(comp[...], inbox[i], preferred_element_type=jnp.float32).astype(jnp.bfloat16)
        if s < days:
            zout[u, s] = packed
            pass_on(u, s).start()
        else:
            zin[u, day] = packed

    def add_block(u, h):
        n = h * cuts + u
        rows = pl.ds(h * (need4 // 2), need4 // 2)

        def tile_step(t, inner):
            cols = pl.ds(pl.multiple_of(t * tile, 128), tile)
            sums = None
            for d in range(days):
                both = jnp.dot(sel[...], zin[u, d, rows, cols], preferred_element_type=jnp.float32)
                a, b = both[:slots], both[slots : 2 * slots]
                c, e = both[2 * slots : 3 * slots], both[3 * slots :]
                real = a * c + b * e
                imag = b * c - a * e
                inv = lax.rsqrt(jnp.maximum(real * real + imag * imag, FLOOR * FLOOR))
                terms = (real, imag, real * inv, imag * inv)
                sums = terms if sums is None else tuple(x + y for x, y in zip(sums, terms))
            coherence = sums[2] * sums[2] + sums[3] * sums[3]
            real, imag = sums[0] * coherence, sums[1] * coherence
            at = pl.ds(pl.multiple_of(n * width + t * tile, 128), tile)
            cos, sin = turn[day, 0:1, at], turn[day, 1:2, at]
            stack[0:slots, cols] = (real * cos + imag * sin).astype(jnp.bfloat16)
            stack[slots : 2 * slots, cols] = (imag * cos - real * sin).astype(jnp.bfloat16)
            return inner

        lax.fori_loop(0, width // tile, tile_step, 0)
        z = jnp.dot(stack[...], table[...], preferred_element_type=jnp.float32)
        cos, sin = outer[day, n, 0:1, :], outer[day, n, 1:2, :]
        even[...] += cos * z[:slots, :HALF] - sin * z[:slots, HALF:]
        odd[...] += sin * z[slots:, :HALF] + cos * z[slots:, HALF:]

    for i in range(AHEAD):
        give_unit(i)
    for load in loads[1:]:
        load.wait()
    for i in range(units + days):
        u, s = i // days, i % days + 1
        if i + AHEAD < units:
            give_unit(i + AHEAD)
        if i < units:
            relay_unit(i)
        if u and s == days // 2:
            for z in range(1, days):
                pass_on(u - 1, z).wait_recv()
            add_block(u - 1, 0)
        if u and s == days:
            add_block(u - 1, 1)

    for d in range(days):
        rows = slice(d * share, (d + 1) * share)
        part[d] = jnp.concatenate([even[rows], odd[rows]], axis=0).astype(jnp.bfloat16)
    for s in range(1, days):
        hand(s).start()
    shares[day] = part[day]
    for s in range(1, days):
        hand(s).wait_recv()
    total = shares[0].astype(jnp.float32)
    for d in range(1, days):
        total = total + shares[d].astype(jnp.float32)
    out[:, HALF:] = total[:share] - total[share:]
    left = total[:share] + total[share:]
    turned = None
    for _ in range(3):
        high = left.astype(jnp.bfloat16)
        left = left - high.astype(jnp.float32)
        piece = jnp.dot(high, flip[...], preferred_element_type=jnp.float32)
        turned = piece if turned is None else turned + piece
    out[:, :HALF] = turned

    for s in range(1, days):
        hand(s).wait_send()
        for u in range(cuts):
            pass_on(u, s).wait_send()
    for i in range(units):
        for p in range(1, holders):
            give(i, p).wait_send()


def shards(days, holders, spectra, station_row, needed, pair_list, counts):
    stations = spectra.shape[2]
    bins = spectra.shape[3]
    need = needed.shape[0]
    slots = pair_list.shape[0]
    cuts = CUTS
    units = cuts * days
    block = bins // days // 2 // cuts
    names = jnp.arange(station_row.shape[0], dtype=jnp.int32)
    my_rows = jnp.sum(jnp.where(needed[:, None] == names[None, :], station_row[None, :], 0), axis=1)
    owner = my_rows // stations
    local = my_rows % stations
    places = jnp.arange(need, dtype=jnp.int32)
    earlier = places[None, :] < places[:, None]
    rank = jnp.sum(jnp.logical_and(owner[:, None] == owner[None, :], earlier), axis=1).astype(jnp.int32)
    my_slot = owner * CAP + rank

    where_is = jnp.arange(holders * CAP, dtype=jnp.int32)
    asked = jnp.sum(jnp.where(where_is[:, None] == my_slot[None, :], local[None, :] + 1, 0), axis=1) - 1
    asked = asked.reshape(holders, 1, CAP)
    quarter = jnp.arange(4, dtype=jnp.int32)
    req = jnp.where(asked >= 0, quarter[None, :, None] * stations + asked, -1)
    req = jnp.broadcast_to(req.reshape(holders * 16, 1), (holders * 16, 4 * stations))

    comp = (owner * 16 + rank)[None, :] + (quarter * CAP)[:, None]
    comp = comp.reshape(4 * need, 1) == jnp.arange(holders * 16, dtype=jnp.int32)[None, :]
    comp = comp.astype(jnp.bfloat16)
    kinds = pair_list.T[:, None, :] + (jnp.arange(2, dtype=jnp.int32) * need)[None, :, None]
    sel = kinds.reshape(4 * slots, 1) == jnp.arange(2 * need, dtype=jnp.int32)[None, :]
    sel = sel.astype(jnp.bfloat16)

    table, outer, turn = lag_constants(bins, days, block)
    bf, f32 = jnp.bfloat16, jnp.float32
    dma = pltpu.SemaphoreType.DMA
    vmem = pl.BlockSpec(memory_space=pltpu.VMEM)
    hbm = pl.BlockSpec(memory_space=pl.ANY)
    summed = pl.pallas_call(
        functools.partial(kernel, holders, days, cuts),
        out_shape=jax.ShapeDtypeStruct((slots // days, LAGS), f32),
        in_specs=[hbm, vmem, vmem, vmem, hbm, hbm, hbm],
        out_specs=vmem,
        scratch_shapes=[
            pltpu.VMEM(spectra.shape[1:], bf),
            pltpu.VMEM(table.shape, bf),
            pltpu.VMEM(outer.shape, f32),
            pltpu.VMEM(turn.shape, f32),
            pltpu.VMEM((holders * 16, 4 * stations), jnp.int32),
            pltpu.VMEM((units, holders * 16, block), bf),
            pltpu.VMEM((units, holders * 16, block), bf),
            pltpu.VMEM((cuts, days, 4 * need, block), bf),
            pltpu.VMEM((cuts, days, 4 * need, block), bf),
            pltpu.VMEM((2 * slots, block), bf),
            pltpu.VMEM((slots, HALF), f32),
            pltpu.VMEM((slots, HALF), f32),
            pltpu.VMEM((HALF, HALF), bf),
            pltpu.VMEM((days, 2 * slots // days, HALF), bf),
            pltpu.VMEM((days, 2 * slots // days, HALF), bf),
            dma((4,)),
            dma((holders,)), dma((holders,)),
            dma((units, holders)), dma((units, holders)),
            dma((cuts, days)), dma((cuts, days)),
            dma((days,)), dma((days,)),
        ],
        compiler_params=pltpu.CompilerParams(
            collective_id=0, has_side_effects=True, vmem_limit_bytes=48 * 2**20
        ),
    )(spectra[0], req, comp, sel, jnp.asarray(table), jnp.asarray(outer), jnp.asarray(turn))
    share = slots // days
    mine = lax.axis_index("day") * share + jnp.arange(share, dtype=jnp.int32)
    scale = 8.0 / math.sqrt(bins) / float(days) ** 3
    return jnp.where((mine < counts[0])[:, None], summed * scale, 0.0)


def solution(mesh):
    in_specs = (P("day", None, "pairs", None), P(), P("pairs"), P("pairs", None), P("pairs"))
    out_specs = P(("pairs", "day"), None)
    body = functools.partial(shards, mesh.shape["day"], mesh.shape["pairs"])
    return jax.shard_map(body, mesh=mesh, in_specs=in_specs, out_specs=out_specs, check_vma=False)
```

```python
import functools
import math

import jax
import jax.numpy as jnp
import numpy as np
from jax import lax
from jax.experimental import pallas as pl
from jax.experimental.pallas import tpu as pltpu
from jax.sharding import PartitionSpec as P

LAGS = 1024
KLO = 720
NFFT = 72000
CAP = 4
HALF = LAGS // 2
FLOOR = 0.25
CUTS = 3
AHEAD = 4
MESH = pl.DeviceIdType.MESH


def lag_constants(bins, days, block):
    odd = 2 * np.arange(HALF, dtype=np.int64) + 1

    def angle(steps):
        return (np.mod(steps, 2 * NFFT) * (math.pi / NFFT)).astype(np.float64)

    inner = angle(np.arange(block, dtype=np.int64)[:, None] * odd[None, :])
    table = np.concatenate([np.cos(inner), np.sin(inner)], axis=1).astype(jnp.bfloat16)
    starts = KLO + np.arange(0, bins, block, dtype=np.int64)
    outer = angle(starts[:, None] * odd[None, :])
    outer = np.stack([np.cos(outer), np.sin(outer)], axis=1).astype(np.float32)
    turn = angle(KLO + np.arange(bins, dtype=np.int64))
    turn = np.stack([np.cos(turn), np.sin(turn)]).astype(np.float32)
    turn = turn.reshape(2, days, bins // days).transpose(1, 0, 2)
    return table, outer.reshape(days, -1, 2, HALF), turn


def kernel(
    holders, days, cuts, spec_hbm, req, comp, sel, table_hbm, outer_hbm, turn_hbm, out,
    spec, table, outer, turn, reqin, outbox, inbox, zout, zin, stack, even, odd, flip, part, shares,
    lsem, qsend, qrecv, xsend, xrecv, zsend, zrecv, rsend, rrecv,
):
    me, day = lax.axis_index("pairs"), lax.axis_index("day")
    width = outbox.shape[2]
    need4 = zin.shape[2]
    slots = even.shape[0]
    share = slots // days
    units = cuts * days
    tile = 256 if width % 256 == 0 else 128

    def xy(p):
        return lax.rem(me + p, holders)

    def zz(s):
        return lax.rem(day + s, days)

    def rows16(b):
        return pl.ds(pl.multiple_of(b * 16, 16), 16)

    def remote(src, dst, ssem, rsem, dev):
        return pltpu.make_async_remote_copy(
            src_ref=src, dst_ref=dst, send_sem=ssem, recv_sem=rsem, device_id=dev, device_id_type=MESH
        )

    def ask(p):
        return remote(req.at[rows16(xy(p))], reqin.at[rows16(me)], qsend.at[p], qrecv.at[p], (xy(p), day))

    def give(i, p):
        return remote(
            outbox.at[i, rows16(xy(p))], inbox.at[i, rows16(me)], xsend.at[i, p], xrecv.at[i, p], (xy(p), day)
        )

    def pass_on(u, s):
        return remote(zout.at[u, s], zin.at[u, day], zsend.at[u, s], zrecv.at[u, s], (me, zz(s)))

    def hand(s):
        return remote(part.at[zz(s)], shares.at[day], rsend.at[s], rrecv.at[s], (me, zz(s)))

    loads = [
        pltpu.make_async_copy(src, dst, lsem.at[i])
        for i, (src, dst) in enumerate(
            ((spec_hbm, spec), (table_hbm, table), (outer_hbm, outer), (turn_hbm, turn))
        )
    ]
    for load in loads:
        load.start()

    barrier = pltpu.get_barrier_semaphore()
    for p in range(1, holders):
        pl.semaphore_signal(barrier, inc=1, device_id=(xy(p), day), device_id_type=MESH)
    for s in range(1, days):
        pl.semaphore_signal(barrier, inc=1, device_id=(me, zz(s)), device_id_type=MESH)
    pl.semaphore_wait(barrier, holders + days - 2)

    for p in range(1, holders):
        ask(p).start()
    reqin[rows16(me)] = req[rows16(me)]
    across = lax.broadcasted_iota(jnp.int32, (HALF, HALF), 0) + lax.broadcasted_iota(jnp.int32, (HALF, HALF), 1)
    flip[...] = jnp.where(across == HALF - 1, 1.0, 0.0).astype(jnp.bfloat16)
    even[...] = jnp.zeros_like(even)
    odd[...] = jnp.zeros_like(odd)
    loads[0].wait()
    for p in range(1, holders):
        ask(p).wait()
    lanes = lax.broadcasted_iota(jnp.int32, reqin.shape, 1)
    pick = jnp.where(reqin[...] == lanes, 1.0, 0.0).astype(jnp.bfloat16)

    def give_unit(i):
        u, s = i // days, i % days + 1
        parts = []
        for h in range(2):
            at = ((2 * zz(s) + h) * cuts + u) * width
            for c in range(2):
                parts.append(spec[c, :, pl.ds(pl.multiple_of(at, 128), width)])
        picked = jnp.dot(pick, jnp.concatenate(parts, axis=0), preferred_element_type=jnp.float32)
        outbox[i] = picked.astype(jnp.bfloat16)
        for p in range(1, holders):
            give(i, p).start()
        inbox[i, rows16(me)] = outbox[i, rows16(me)]

    def relay_unit(i):
        u, s = i // days, i % days + 1
        for p in range(1, holders):
            give(i, p).wait_recv()
        packed = jnp.dot(comp[...], inbox[i], preferred_element_type=jnp.float32).astype(jnp.bfloat16)
        if s < days:
            zout[u, s] = packed
            pass_on(u, s).start()
        else:
            zin[u, day] = packed

    def add_block(u, h):
        n = h * cuts + u
        rows = pl.ds(h * (need4 // 2), need4 // 2)

        def tile_step(t, inner):
            cols = pl.ds(pl.multiple_of(t * tile, 128), tile)
            sums = None
            for d in range(days):
                both = jnp.dot(sel[...], zin[u, d, rows, cols], preferred_element_type=jnp.float32)
                a, b = both[:slots], both[slots : 2 * slots]
                c, e = both[2 * slots : 3 * slots], both[3 * slots :]
                real = a * c + b * e
                imag = b * c - a * e
                inv = lax.rsqrt(jnp.maximum(real * real + imag * imag, FLOOR * FLOOR))
                terms = (real, imag, real * inv, imag * inv)
                sums = terms if sums is None else tuple(x + y for x, y in zip(sums, terms))
            coherence = sums[2] * sums[2] + sums[3] * sums[3]
            real, imag = sums[0] * coherence, sums[1] * coherence
            at = pl.ds(pl.multiple_of(n * width + t * tile, 128), tile)
            cos, sin = turn[day, 0:1, at], turn[day, 1:2, at]
            stack[0:slots, cols] = (real * cos + imag * sin).astype(jnp.bfloat16)
            stack[slots : 2 * slots, cols] = (imag * cos - real * sin).astype(jnp.bfloat16)
            return inner

        lax.fori_loop(0, width // tile, tile_step, 0)
        z = jnp.dot(stack[...], table[...], preferred_element_type=jnp.float32)
        cos, sin = outer[day, n, 0:1, :], outer[day, n, 1:2, :]
        even[...] += cos * z[:slots, :HALF] - sin * z[:slots, HALF:]
        odd[...] += sin * z[slots:, :HALF] + cos * z[slots:, HALF:]

    for i in range(AHEAD):
        give_unit(i)
    for load in loads[1:]:
        load.wait()
    for i in range(units + days):
        u, s = i // days, i % days + 1
        if i + AHEAD < units:
            give_unit(i + AHEAD)
        if i < units:
            relay_unit(i)
        if u and s == days // 2:
            for z in range(1, days):
                pass_on(u - 1, z).wait_recv()
            add_block(u - 1, 0)
        if u and s == days:
            add_block(u - 1, 1)

    for d in range(days):
        rows = slice(d * share, (d + 1) * share)
        part[d] = jnp.concatenate([even[rows], odd[rows]], axis=0).astype(jnp.bfloat16)
    for s in range(1, days):
        hand(s).start()
    shares[day] = part[day]
    for s in range(1, days):
        hand(s).wait_recv()
    total = shares[0].astype(jnp.float32)
    for d in range(1, days):
        total = total + shares[d].astype(jnp.float32)
    out[:, HALF:] = total[:share] - total[share:]
    left = total[:share] + total[share:]
    turned = None
    for _ in range(3):
        high = left.astype(jnp.bfloat16)
        left = left - high.astype(jnp.float32)
        piece = jnp.dot(high, flip[...], preferred_element_type=jnp.float32)
        turned = piece if turned is None else turned + piece
    out[:, :HALF] = turned

    for s in range(1, days):
        hand(s).wait_send()
        for u in range(cuts):
            pass_on(u, s).wait_send()
    for i in range(units):
        for p in range(1, holders):
            give(i, p).wait_send()


def shards(days, holders, spectra, station_row, needed, pair_list, counts):
    stations = spectra.shape[2]
    bins = spectra.shape[3]
    need = needed.shape[0]
    slots = pair_list.shape[0]
    cuts = CUTS
    units = cuts * days
    block = bins // days // 2 // cuts
    names = jnp.arange(station_row.shape[0], dtype=jnp.int32)
    my_rows = jnp.sum(jnp.where(needed[:, None] == names[None, :], station_row[None, :], 0), axis=1)
    owner = my_rows // stations
    local = my_rows % stations
    places = jnp.arange(need, dtype=jnp.int32)
    earlier = places[None, :] < places[:, None]
    rank = jnp.sum(jnp.logical_and(owner[:, None] == owner[None, :], earlier), axis=1).astype(jnp.int32)
    my_slot = owner * CAP + rank

    where_is = jnp.arange(holders * CAP, dtype=jnp.int32)
    asked = jnp.sum(jnp.where(where_is[:, None] == my_slot[None, :], local[None, :] + 1, 0), axis=1) - 1
    asked = asked.reshape(holders, 1, CAP)
    quarter = jnp.arange(4, dtype=jnp.int32)
    req = jnp.where(asked >= 0, quarter[None, :, None] * stations + asked, -1)
    req = jnp.broadcast_to(req.reshape(holders * 16, 1), (holders * 16, 4 * stations))

    comp = (owner * 16 + rank)[None, :] + (quarter * CAP)[:, None]
    comp = comp.reshape(4 * need, 1) == jnp.arange(holders * 16, dtype=jnp.int32)[None, :]
    comp = comp.astype(jnp.bfloat16)
    kinds = pair_list.T[:, None, :] + (jnp.arange(2, dtype=jnp.int32) * need)[None, :, None]
    sel = kinds.reshape(4 * slots, 1) == jnp.arange(2 * need, dtype=jnp.int32)[None, :]
    sel = sel.astype(jnp.bfloat16)

    table, outer, turn = lag_constants(bins, days, block)
    bf, f32 = jnp.bfloat16, jnp.float32
    dma = pltpu.SemaphoreType.DMA
    vmem = pl.BlockSpec(memory_space=pltpu.VMEM)
    hbm = pl.BlockSpec(memory_space=pl.ANY)
    summed = pl.pallas_call(
        functools.partial(kernel, holders, days, cuts),
        out_shape=jax.ShapeDtypeStruct((slots // days, LAGS), f32),
        in_specs=[hbm, vmem, vmem, vmem, hbm, hbm, hbm],
        out_specs=vmem,
        scratch_shapes=[
            pltpu.VMEM(spectra.shape[1:], bf),
            pltpu.VMEM(table.shape, bf),
            pltpu.VMEM(outer.shape, f32),
            pltpu.VMEM(turn.shape, f32),
            pltpu.VMEM((holders * 16, 4 * stations), jnp.int32),
            pltpu.VMEM((units, holders * 16, block), bf),
            pltpu.VMEM((units, holders * 16, block), bf),
            pltpu.VMEM((cuts, days, 4 * need, block), bf),
            pltpu.VMEM((cuts, days, 4 * need, block), bf),
            pltpu.VMEM((2 * slots, block), bf),
            pltpu.VMEM((slots, HALF), f32),
            pltpu.VMEM((slots, HALF), f32),
            pltpu.VMEM((HALF, HALF), bf),
            pltpu.VMEM((days, 2 * slots // days, HALF), bf),
            pltpu.VMEM((days, 2 * slots // days, HALF), bf),
            dma((4,)),
            dma((holders,)), dma((holders,)),
            dma((units, holders)), dma((units, holders)),
            dma((cuts, days)), dma((cuts, days)),
            dma((days,)), dma((days,)),
        ],
        compiler_params=pltpu.CompilerParams(
            collective_id=0, has_side_effects=True, vmem_limit_bytes=63 * 2**20
        ),
    )(spectra[0], req, comp, sel, jnp.asarray(table), jnp.asarray(outer), jnp.asarray(turn))
    share = slots // days
    mine = lax.axis_index("day") * share + jnp.arange(share, dtype=jnp.int32)
    scale = 8.0 / math.sqrt(bins) / float(days) ** 3
    return jnp.where((mine < counts[0])[:, None], summed * scale, 0.0)


def solution(mesh):
    in_specs = (P("day", None, "pairs", None), P(), P("pairs"), P("pairs", None), P("pairs"))
    out_specs = P(("pairs", "day"), None)
    body = functools.partial(shards, mesh.shape["day"], mesh.shape["pairs"])
    return jax.shard_map(body, mesh=mesh, in_specs=in_specs, out_specs=out_specs, check_vma=False)
```
